1024 devices in a mesh: col: 64 (over z, x), row: 16 (over y, core).
Axes of the slice: x: 8, y: 8, z: 8, core: 2. Of those that a mesh axis runs over, the one named last changes fastest.
Arguments:
- weight: float32 [8192, 16384], P('row', 'col'), may hold values from -6 to 6
- momentum: float32 [8192, 16384], P('row', 'col'), may hold values from -6 to 6
- gradient: bfloat16 [8192, 16384], P('row', 'col'), may hold values from -6 to 6
- right_factor: float32 [16384, 256], P('col'), may hold values from -6 to 6
Outputs:
- new_weight: float32 [8192, 16384], P('row', 'col')
- new_momentum: float32 [8192, 16384], P('row', 'col')
- new_factor: float32 [16384, 256], P('col')
The draws below stay inside these ranges and needn't reach their ends.
All inputs are finite; a program needn't handle non-finite values.
Results may differ from the reference program's by a relative error of at most 0.0003.
Values sent between devices are 32-bit elements; how exact they have to be, the bound alone decides.
A program may use at most 32 MiB of HBM per device.

```python
import jax
import jax.numpy as jnp
from jax import lax

D_IN = 16384
ROWS = 8192
RANK = 256


def steps_of(key, extent, split, low, top_value):
    gain, own = 1.0, jax.random.fold_in(key, 6)
    for dim, blocks in split:
        heights = jnp.exp(jax.random.uniform(jax.random.fold_in(own, dim), (blocks,), jnp.float32, low / len(split), top_value / len(split)))
        gain = gain * jnp.repeat(heights, extent[dim] // blocks).reshape([-1 if axis == dim else 1 for axis in range(len(extent))])
    return gain


def noise(stream_key, extent, scale, most, pieces=(), dtype=jnp.bfloat16):
    result = scale * jax.random.normal(stream_key, extent, jnp.float32)
    if pieces:
        result = result * steps_of(stream_key, extent, pieces, -0.22, 0.18)
    return jnp.clip(result, -most, most).astype(dtype)


def setup_inputs(seed: int = 0) -> dict:
    arg_keys = jax.random.split(jax.random.key(seed), 5)
    weight = noise(arg_keys[0], (ROWS, D_IN), 1.0, 6.0, ((0, 16), (1, 64)), jnp.float32)
    momentum = noise(arg_keys[1], (ROWS, D_IN), 1.0, 6.0, ((0, 16), (1, 64)), jnp.float32)
    gradient = noise(arg_keys[2], (ROWS, D_IN), 1.0, 6.0, ((0, 16), (1, 64)))
    right_factor = noise(arg_keys[3], (D_IN, RANK), 1.0, 6.0, ((0, 64),), jnp.float32)
    return {"weight": weight, "momentum": momentum, "gradient": gradient, "right_factor": right_factor}


def matmul(left_side, right_side):
    return jnp.dot(left_side.astype(jnp.float32), right_side.astype(jnp.float32), precision=lax.Precision.HIGHEST, preferred_element_type=jnp.float32)

def reference(weight, momentum, gradient, right_factor):
    combined = momentum + gradient.astype(jnp.float32)
    left_raw = matmul(combined, right_factor)
    gram_matrix = matmul(left_raw.T, left_raw)
    lower = jnp.linalg.cholesky(gram_matrix)
    left_factor = lax.linalg.triangular_solve(lower, left_raw, left_side=False, lower=True, transpose_a=True)
    right_raw = matmul(combined.T, left_factor)
    new_momentum = combined - 0.05 * matmul(left_factor, right_raw.T)
    squares = lax.optimization_barrier(jnp.sum(right_raw * right_raw, axis=0))
    column_scale = jnp.sqrt(squares / D_IN + 1e-06)
    new_factor = right_raw / column_scale
    new_weight = weight - 0.5 * matmul(left_factor, new_factor.T)
    return (new_weight, new_momentum, new_factor)
```

```python
import functools
import math

import jax
import jax.numpy as jnp
from jax import lax
from jax.experimental import pallas as pl
from jax.experimental.pallas import tpu as pltpu
from jax.sharding import PartitionSpec as P

D_IN = 16384
RANK = 256
LANES = 128
MESH = pl.DeviceIdType.MESH
F32 = jnp.float32

OUT_X, OUT_Z, IN_X, IN_Z, BACK_Z, BACK_X, ALL_X, ALL_Z, GRAM, GRAM_ALL, RIGHT, RIGHT_ALL, SQUARES = range(13)


def dot(first, second, first_dim, second_dim):
    return lax.dot_general(
        first,
        second,
        (((first_dim,), (second_dim,)), ((), ())),
        precision=lax.Precision.HIGHEST,
        preferred_element_type=F32,
    )


def iota(shape, dim):
    return lax.broadcasted_iota(jnp.int32, shape, dim)


def inverse_factor(work, block, inner):
    n = work.shape[0]

    def step(index, carry):
        panel = work[0:block, :]
        lane = iota((block, n), 1)
        sub = iota((block, n), 0)
        narrow = iota((block, LANES), 0)
        row_lane = iota((1, n), 1)
        for start in range(0, block, inner):
            columns = [
                jnp.broadcast_to(panel[:, start + j : start + j + 1], (block, LANES)) for j in range(inner)
            ]
            for j in range(inner):
                k = start + j
                scale = lax.rsqrt(columns[j][k : k + 1, :])
                factor = jnp.where(narrow > k, columns[j] * scale, 0.0)
                row = jnp.where(row_lane == k, 1.0, panel[k : k + 1, :])
                row = row * jnp.concatenate([scale] * (n // LANES), axis=1)
                for later in range(j + 1, inner):
                    columns[later] = columns[later] - factor * (columns[later][k : k + 1, :] * scale)
                wide = jnp.concatenate([factor] * (n // LANES), axis=1)
                below = jnp.where((lane == k) & (sub > k), 0.0, panel) - wide * row
                panel = jnp.where(sub == k, jnp.broadcast_to(row, (block, n)), below)
        left = n - block * index
        own = jnp.where((lane > sub) & (lane < left), 0.0, panel)
        right_side = jnp.where((lane < block) & (lane > sub), 0.0, panel)
        left_side = jnp.where((lane < left) & (lane >= block), panel, 0.0)
        update = dot(left_side[:, block:], right_side, 0, 0)
        rest_lane = iota((n - block, n), 1)
        rest_sub = iota((n - block, n), 0) + block
        rest = jnp.where((rest_lane < block) & (rest_sub < left), 0.0, work[block:, :]) - update
        work[0 : n - block, :] = pltpu.roll(rest, n - block, 1)
        work[n - block :, :] = pltpu.roll(own, n - block, 1)
        return carry

    lax.fori_loop(0, n // block, step, 0)


def kernel(
    side, depth, weight_hbm, momentum_hbm, gradient_hbm, factor_hbm, new_weight_hbm, new_momentum_hbm, new_factor_hbm,
    weight, momentum, gradient, factor, combined, partial, scatter_in, middle, middle_in, left, gram, gram_in, gram_all,
    work, right, right_in, right_all, squares, squares_in, new_weight, new_momentum, new_factor,
    load_sem, store_sem, send_sem, recv_sem,
):
    rows = partial.shape[1]
    big, small = rows // side, rows // side // side
    col, row = lax.axis_index("col"), lax.axis_index("row")
    z, x = lax.div(col, side), lax.rem(col, side)
    far = sorted(range(1, side), key=lambda k: -min(k, side - k))
    far_row = sorted(range(1, 2 * depth), key=lambda k: -min(k // 2, depth - k // 2))

    def x_peer(k):
        return lax.rem(x + k, side)

    def z_peer(k):
        return lax.rem(z + k, side)

    def at(z_of, x_of):
        return (z_of * side + x_of, row)

    def row_peer(k):
        return lax.rem(row + k, 2 * depth)

    def send(source, target, batch, device):
        pltpu.make_async_remote_copy(
            src_ref=source,
            dst_ref=target,
            send_sem=send_sem.at[batch],
            recv_sem=recv_sem.at[batch],
            device_id=device,
            device_id_type=MESH,
        ).start()

    def arrived(target, batch):
        pltpu.make_async_copy(target, target, recv_sem.at[batch]).wait()

    def sent(source, batch):
        pltpu.make_async_copy(source, source, send_sem.at[batch]).wait()

    barrier = pltpu.get_barrier_semaphore()
    for k in far:
        pl.semaphore_signal(barrier, inc=1, device_id=at(z, x_peer(k)), device_id_type=MESH)
        pl.semaphore_signal(barrier, inc=1, device_id=at(z_peer(k), x), device_id_type=MESH)
    for k in far_row:
        pl.semaphore_signal(barrier, inc=1, device_id=(col, row_peer(k)), device_id_type=MESH)

    loads = [
        pltpu.make_async_copy(source, target, load_sem.at[i])
        for i, (source, target) in enumerate(
            ((momentum_hbm, momentum), (gradient_hbm, gradient), (factor_hbm, factor), (weight_hbm, weight))
        )
    ]
    for load in loads:
        load.start()
    for load in loads[:3]:
        load.wait()
    combined[...] = momentum[...] + gradient[...].astype(F32)
    product = dot(combined[...], factor[...], 1, 0)
    partial[0] = product[:, :LANES]
    partial[1] = product[:, LANES:]

    pl.semaphore_wait(barrier, 2 * len(far) + len(far_row))

    for k in far:
        send(partial.at[0, pl.ds(x_peer(k) * big, big)], scatter_in.at[0, k], OUT_X, at(z, x_peer(k)))
        send(partial.at[1, pl.ds(z_peer(k) * big, big)], scatter_in.at[1, k], OUT_Z, at(z_peer(k), x))
    arrived(scatter_in.at[0, pl.ds(1, side - 1)], OUT_X)
    middle[0] = partial[0, pl.ds(x * big, big)] + jnp.sum(scatter_in[0, 1:], axis=0)
    for k in far:
        send(middle.at[0, pl.ds(z_peer(k) * small, small)], middle_in.at[0, k], IN_Z, at(z_peer(k), x))
    arrived(scatter_in.at[1, pl.ds(1, side - 1)], OUT_Z)
    middle[1] = partial[1, pl.ds(z * big, big)] + jnp.sum(scatter_in[1, 1:], axis=0)
    for k in far:
        send(middle.at[1, pl.ds(x_peer(k) * small, small)], middle_in.at[1, k], IN_X, at(z, x_peer(k)))

    first = pl.ds(x * big + z * small, small)
    second = pl.ds(z * big + x * small, small)
    arrived(middle_in.at[0, pl.ds(1, side - 1)], IN_Z)
    left[0, first] = middle[0, pl.ds(z * small, small)] + jnp.sum(middle_in[0, 1:], axis=0)
    for k in far:
        send(left.at[0, first], left.at[0, first], BACK_Z, at(z_peer(k), x))
    arrived(middle_in.at[1, pl.ds(1, side - 1)], IN_X)
    left[1, second] = middle[1, pl.ds(x * small, small)] + jnp.sum(middle_in[1, 1:], axis=0)
    for k in far:
        send(left.at[1, second], left.at[1, second], BACK_X, at(z, x_peer(k)))
    arrived(left.at[0, pl.ds(0, big - small)], BACK_Z)
    for k in far:
        block = pl.ds(x * big, big)
        send(left.at[0, block], left.at[0, block], ALL_X, at(z, x_peer(k)))
    arrived(left.at[1, pl.ds(0, big - small)], BACK_X)
    for k in far:
        block = pl.ds(z * big, big)
        send(left.at[1, block], left.at[1, block], ALL_Z, at(z_peer(k), x))
    arrived(left.at[0, pl.ds(0, rows - big)], ALL_X)
    arrived(left.at[1, pl.ds(0, rows - big)], ALL_Z)

    left_raw = jnp.concatenate([left[0], left[1]], axis=1)
    gram[0:RANK] = dot(left_raw, left[0], 0, 0)
    gram[RANK:] = dot(left_raw, left[1], 0, 0)
    tile_rows = 2 * RANK // (side * side)
    tile = pl.ds(col * tile_rows, tile_rows)
    gram_in[row] = gram[tile]
    for k in far_row:
        send(gram.at[tile], gram_in.at[row], GRAM, (col, row_peer(k)))

    right[...] = dot(combined[...], left_raw, 0, 0)
    strip_rows = RANK // (2 * depth)
    strip = pl.ds(row * strip_rows, strip_rows)
    for k in far_row:
        send(right.at[pl.ds(row_peer(k) * strip_rows, strip_rows)], right_in.at[k], RIGHT, (col, row_peer(k)))

    arrived(gram_in.at[pl.ds(0, 2 * depth - 1)], GRAM)
    gram_all[tile] = jnp.sum(gram_in[...], axis=0)

    def plane(start):
        def one(j, carry):
            dz, dx = far_of(lax.div(j, side)), far_of(lax.rem(j, side))
            start(at(lax.rem(z + dz, side), lax.rem(x + dx, side)))
            return carry

        lax.fori_loop(0, side * side - 1, one, 0)

    def far_of(j):
        half = lax.div(j + 1, 2)
        return side // 2 + jnp.where(lax.rem(j, 2) == 1, -half, half)

    plane(lambda device: send(gram_all.at[tile], gram_all.at[tile], GRAM_ALL, device))

    arrived(right_in.at[pl.ds(1, 2 * depth - 1)], RIGHT)
    right_all[strip] = right[strip] + jnp.sum(right_in[1:], axis=0)
    for k in far_row:
        send(right_all.at[strip], right_all.at[strip], RIGHT_ALL, (col, row_peer(k)))

    arrived(gram_all.at[pl.ds(0, 2 * RANK - tile_rows)], GRAM_ALL)
    work[:, :LANES] = gram_all[0:RANK]
    work[:, LANES:] = gram_all[RANK:]
    inverse_factor(work, 64, 16)
    inverse = work[...]

    arrived(right_all.at[pl.ds(0, RANK - strip_rows)], RIGHT_ALL)
    right_raw = dot(right_all[...], inverse, 1, 1)
    sums = jnp.sum(right_raw * right_raw, axis=0, keepdims=True)
    squares[...] = jnp.zeros_like(squares)
    squares[0:1] = sums[:, :LANES]
    squares[1:2] = sums[:, LANES:]
    squares_in[col] = squares[...]
    plane(lambda device: send(squares, squares_in.at[col], SQUARES, device))

    left_factor = dot(left_raw, inverse, 1, 1)
    new_momentum[...] = combined[...] - 0.05 * dot(left_factor, right_raw, 1, 1)
    store_momentum = pltpu.make_async_copy(new_momentum, new_momentum_hbm, store_sem.at[0])
    store_momentum.start()
    loads[3].wait()

    arrived(squares_in.at[pl.ds(0, side * side - 1)], SQUARES)
    total = jnp.sum(squares_in[...], axis=0)
    total = jnp.concatenate([total[0:1], total[1:2]], axis=1)
    new_factor[...] = right_raw / jnp.sqrt(total / D_IN + 1e-06)
    store_factor = pltpu.make_async_copy(new_factor, new_factor_hbm, store_sem.at[1])
    store_factor.start()
    new_weight[...] = weight[...] - 0.5 * dot(left_factor, new_factor[...], 1, 1)
    store_weight = pltpu.make_async_copy(new_weight, new_weight_hbm, store_sem.at[2])
    store_weight.start()

    sent(scatter_in.at[0, pl.ds(1, side - 1)], OUT_X)
    sent(scatter_in.at[1, pl.ds(1, side - 1)], OUT_Z)
    sent(middle_in.at[0, pl.ds(1, side - 1)], IN_Z)
    sent(middle_in.at[1, pl.ds(1, side - 1)], IN_X)
    sent(left.at[0, pl.ds(0, big - small)], BACK_Z)
    sent(left.at[1, pl.ds(0, big - small)], BACK_X)
    sent(left.at[0, pl.ds(0, rows - big)], ALL_X)
    sent(left.at[1, pl.ds(0, rows - big)], ALL_Z)
    sent(gram_in.at[pl.ds(0, 2 * depth - 1)], GRAM)
    sent(gram_all.at[pl.ds(0, 2 * RANK - tile_rows)], GRAM_ALL)
    sent(right_in.at[pl.ds(1, 2 * depth - 1)], RIGHT)
    sent(right_all.at[pl.ds(0, RANK - strip_rows)], RIGHT_ALL)
    sent(squares_in.at[pl.ds(0, side * side - 1)], SQUARES)
    store_momentum.wait()
    store_factor.wait()
    store_weight.wait()


def on_device(side, depth, weight, momentum, gradient, right_factor):
    rows, columns = weight.shape
    big, small = rows // side, rows // side // side
    vmem = pltpu.VMEM
    scratch = [
        vmem((rows, columns), F32),
        vmem((rows, columns), F32),
        vmem((rows, columns), gradient.dtype),
        vmem((columns, RANK), F32),
        vmem((rows, columns), F32),
        vmem((2, rows, LANES), F32),
        vmem((2, side, big, LANES), F32),
        vmem((2, big, LANES), F32),
        vmem((2, side, small, LANES), F32),
        vmem((2, rows, LANES), F32),
        vmem((2 * RANK, LANES), F32),
        vmem((2 * depth, 2 * RANK // (side * side), LANES), F32),
        vmem((2 * RANK, LANES), F32),
        vmem((RANK, RANK), F32),
        vmem((columns, RANK), F32),
        vmem((2 * depth, columns // (2 * depth), RANK), F32),
        vmem((columns, RANK), F32),
        vmem((8, LANES), F32),
        vmem((side * side, 8, LANES), F32),
        vmem((rows, columns), F32),
        vmem((rows, columns), F32),
        vmem((columns, RANK), F32),
        pltpu.SemaphoreType.DMA((4,)),
        pltpu.SemaphoreType.DMA((3,)),
        pltpu.SemaphoreType.DMA((13,)),
        pltpu.SemaphoreType.DMA((13,)),
    ]
    return pl.pallas_call(
        functools.partial(kernel, side, depth),
        out_shape=(
            jax.ShapeDtypeStruct((rows, columns), F32),
            jax.ShapeDtypeStruct((rows, columns), F32),
            jax.ShapeDtypeStruct((columns, RANK), F32),
        ),
        in_specs=[pl.BlockSpec(memory_space=pl.ANY)] * 4,
        out_specs=(pl.BlockSpec(memory_space=pl.ANY),) * 3,
        scratch_shapes=scratch,
        compiler_params=pltpu.CompilerParams(
            collective_id=0, has_side_effects=True, vmem_limit_bytes=48 * 1024 * 1024
        ),
        name="dion_step",
    )(weight, momentum, gradient, right_factor)


def solution(mesh):
    side = math.isqrt(mesh.shape["col"])
    depth = mesh.shape["row"] // 2
    in_specs = (P("row", "col"), P("row", "col"), P("row", "col"), P("col", None))
    out_specs = (P("row", "col"), P("row", "col"), P("col", None))
    return jax.shard_map(
        functools.partial(on_device, side, depth), mesh=mesh, in_specs=in_specs, out_specs=out_specs, check_vma=False
    )
```

```python
import functools
import math

import jax
import jax.numpy as jnp
from jax import lax
from jax.experimental import pallas as pl
from jax.experimental.pallas import tpu as pltpu
from jax.sharding import PartitionSpec as P

D_IN = 16384
RANK = 256
LANES = 128
MESH = pl.DeviceIdType.MESH
F32 = jnp.float32

FAR_X, NEAR_X, FAR_Z, NEAR_Z, IN_X, IN_Z, BACK_X, BACK_Z = 0, 1, 2, 3, 4, 5, 6, 9
ALL_X, ALL_Z, GRAM, GRAM_FIRST, GRAM_REST, RIGHT, RIGHT_ALL, SQUARES, BATCHES = range(12, 21)


def dot(first, second, first_dim, second_dim):
    return lax.dot_general(
        first,
        second,
        (((first_dim,), (second_dim,)), ((), ())),
        precision=lax.Precision.HIGHEST,
        preferred_element_type=F32,
    )


def iota(shape, dim):
    return lax.broadcasted_iota(jnp.int32, shape, dim)


def inverse_factor(work, block, inner, fill_rest):
    n = work.shape[0]

    def step(index, carry):
        panel = work[0:block, :]
        lane = iota((block, n), 1)
        sub = iota((block, n), 0)
        narrow = iota((block, LANES), 0)
        row_lane = iota((1, n), 1)
        for start in range(0, block, inner):
            columns = [
                jnp.broadcast_to(panel[:, start + j : start + j + 1], (block, LANES)) for j in range(inner)
            ]
            for j in range(inner):
                k = start + j
                scale = lax.rsqrt(columns[j][k : k + 1, :])
                factor = jnp.where(narrow > k, columns[j] * scale, 0.0)
                row = jnp.where(row_lane == k, 1.0, panel[k : k + 1, :])
                row = row * jnp.concatenate([scale] * (n // LANES), axis=1)
                for later in range(j + 1, inner):
                    columns[later] = columns[later] - factor * (columns[later][k : k + 1, :] * scale)
                wide = jnp.concatenate([factor] * (n // LANES), axis=1)
                below = jnp.where((lane == k) & (sub > k), 0.0, panel) - wide * row
                panel = jnp.where(sub == k, jnp.broadcast_to(row, (block, n)), below)
        pl.when(index == 0)(fill_rest)
        left = n - block * index
        own = jnp.where((lane > sub) & (lane < left), 0.0, panel)
        right_side = jnp.where((lane < block) & (lane > sub), 0.0, panel)
        left_side = jnp.where((lane < left) & (lane >= block), panel, 0.0)
        update = dot(left_side[:, block:], right_side, 0, 0)
        rest_lane = iota((n - block, n), 1)
        rest_sub = iota((n - block, n), 0) + block
        rest = jnp.where((rest_lane < block) & (rest_sub < left), 0.0, work[block:, :]) - update
        work[0 : n - block, :] = pltpu.roll(rest, n - block, 1)
        work[n - block :, :] = pltpu.roll(own, n - block, 1)
        return carry

    lax.fori_loop(0, n // block, step, 0)


def kernel(
    side, depth, weight_hbm, momentum_hbm, gradient_hbm, factor_hbm,
    weight, new_momentum, left_factor, right_raw, total,
    momentum, gradient, factor, combined, product, partial, scatter_in, middle, middle_in, gathered, left, gram, gram_in,
    gram_all, work, right, right_in, right_all, squares, squares_in, load_sem, send_sem, recv_sem,
):
    col, row = lax.axis_index("col"), lax.axis_index("row")
    z, x = lax.div(col, side), lax.rem(col, side)
    here, half = (x, z), side // 2
    far = sorted(range(1, side), key=lambda k: -min(k, side - k))
    far_row = sorted(range(1, 2 * depth), key=lambda k: -min(k // 2, depth - k // 2))

    def x_peer(k):
        return at(z, lax.rem(x + k, side))

    def z_peer(k):
        return at(lax.rem(z + k, side), x)

    def at(z_of, x_of):
        return (z_of * side + x_of, row)

    def row_peer(k):
        return lax.rem(row + k, 2 * depth)

    def send(source, target, batch, device):
        pltpu.make_async_remote_copy(
            src_ref=source,
            dst_ref=target,
            send_sem=send_sem.at[batch],
            recv_sem=recv_sem.at[batch],
            device_id=device,
            device_id_type=MESH,
        ).start()

    def arrived(target, batch):
        pltpu.make_async_copy(target, target, recv_sem.at[batch]).wait()

    def sent(source, batch):
        pltpu.make_async_copy(source, source, send_sem.at[batch]).wait()

    barrier = pltpu.get_barrier_semaphore()
    for k in far:
        pl.semaphore_signal(barrier, inc=1, device_id=x_peer(k), device_id_type=MESH)
        pl.semaphore_signal(barrier, inc=1, device_id=z_peer(k), device_id_type=MESH)
    for k in far_row:
        pl.semaphore_signal(barrier, inc=1, device_id=(col, row_peer(k)), device_id_type=MESH)

    loads = [
        pltpu.make_async_copy(source, target, load_sem.at[i])
        for i, (source, target) in enumerate(
            ((momentum_hbm, momentum), (gradient_hbm, gradient), (factor_hbm, factor), (weight_hbm, weight))
        )
    ]
    for load in loads:
        load.start()
    for load in loads[:3]:
        load.wait()
    combined[...] = momentum[...] + gradient[...].astype(F32)
    whole = dot(combined[...], factor[...], 1, 0)
    tiles = product.shape[1:]
    product[0] = whole[:, :LANES].reshape(tiles)
    product[1] = whole[:, LANES:].reshape(tiles)

    def place(part, o):
        return lax.rem(here[1 - part] + o + side - 1, side)

    for o in range(side):
        partial[0, :, o] = product[0, :, place(0, o)]
        partial[1, o] = product[1, place(1, o)]

    pl.semaphore_wait(barrier, 2 * len(far) + len(far_row))

    def scatter(low, batch_x, batch_z):
        tiles = pl.ds(low, half)
        for k in far:
            send(partial.at[0, lax.rem(x + k, side), tiles], scatter_in.at[0, k, tiles], batch_x, x_peer(k))
            send(partial.at[1, tiles, lax.rem(z + k, side)], scatter_in.at[1, k, tiles], batch_z, z_peer(k))

    def reduce_on(low, part, batch):
        tiles = pl.ds(low, half)
        arrived(scatter_in.at[part, pl.ds(1, side - 1), tiles], batch)
        own = partial[0, x, tiles] if part == 0 else partial[1, tiles, z]
        middle[part, tiles] = own + jnp.sum(scatter_in[part, 1:, tiles], axis=0)
        peer, onward = (z_peer, IN_Z) if part == 0 else (x_peer, IN_X)
        for k in far:
            o = (k + 1) % side
            if low <= o < low + half:
                send(middle.at[part, o], middle_in.at[part, k], onward, peer(k))

    scatter(half, FAR_X, FAR_Z)
    scatter(0, NEAR_X, NEAR_Z)
    reduce_on(half, 0, FAR_X)
    reduce_on(half, 1, FAR_Z)
    reduce_on(0, 0, NEAR_X)
    reduce_on(0, 1, NEAR_Z)

    groups = [(0, min(3, side)), (min(3, side), half + 1), (half + 1, side)]
    groups = [(low, high) for low, high in groups if high > low]

    def group_of(o):
        return next(g for g, (low, high) in enumerate(groups) if low <= o < high)

    def count(g):
        return sum(1 for o in range(*groups[g]) if o != 1)

    for part, batch, back, peer in ((0, IN_Z, BACK_Z, z_peer), (1, IN_X, BACK_X, x_peer)):
        arrived(middle_in.at[part, pl.ds(1, side - 1)], batch)
        gathered[part, here[part], 1] = middle[part, 1] + jnp.sum(middle_in[part, 1:], axis=0)
        for k in far:
            o = (1 - k) % side
            send(
                gathered.at[part, here[part], 1], gathered.at[part, here[part], o], back + group_of(o), peer(k)
            )
    for g, (low, high) in enumerate(groups):
        for part, back, batch, peer in ((0, BACK_Z, ALL_X, x_peer), (1, BACK_X, ALL_Z, z_peer)):
            if count(g):
                arrived(middle_in.at[part, pl.ds(0, count(g))], back + g)
            block = gathered.at[part, here[part], pl.ds(low, high - low)]
            for k in far:
                send(block, block, batch, peer(k))
    arrived(gathered.at[0, pl.ds(1, side - 1)], ALL_X)
    arrived(gathered.at[1, pl.ds(1, side - 1)], ALL_Z)
    for o in range(side):
        left[0, :, place(0, o)] = gathered[0, :, o]
        left[1, place(1, o)] = gathered[1, :, o]

    rows = combined.shape[0]
    halves = [left[part].reshape(rows, LANES) for part in range(2)]
    left_raw = jnp.concatenate(halves, axis=1)
    tile_rows = 2 * RANK // (side * side)
    tile = pl.ds(col * tile_rows, tile_rows)
    start = col * tile_rows
    block_row = lax.rem(lax.div(start, LANES), 2)
    block_col = lax.div(start, RANK)
    gram[...] = dot(left[block_row].reshape(rows, LANES), left[block_col].reshape(rows, LANES), 0, 0)
    own_tile = pl.ds(lax.rem(start, LANES), tile_rows)
    gram_in[row] = gram[own_tile]
    for k in far_row:
        send(gram.at[own_tile], gram_in.at[row], GRAM, (col, row_peer(k)))

    right[...] = dot(combined[...], left_raw, 0, 0)
    strip_rows = RANK // (2 * depth)
    strip = pl.ds(row * strip_rows, strip_rows)
    for k in far_row:
        send(right.at[pl.ds(row_peer(k) * strip_rows, strip_rows)], right_in.at[k], RIGHT, (col, row_peer(k)))

    arrived(gram_in.at[pl.ds(0, 2 * depth - 1)], GRAM)
    gram_in[0] = jnp.sum(gram_in[...], axis=0)

    def plane(start):
        def one(j, carry):
            dz, dx = far_of(lax.div(j, side)), far_of(lax.rem(j, side))
            start(at(lax.rem(z + dz, side), lax.rem(x + dx, side)))
            return carry

        lax.fori_loop(0, side * side - 1, one, 0)

    def far_of(j):
        step = lax.div(j + 1, 2)
        return half + jnp.where(lax.rem(j, 2) == 1, -step, step)

    panel_rows = RANK // 4
    first = lax.rem(start, RANK) < panel_rows
    gram_batch = jnp.where(first, GRAM_FIRST, GRAM_REST)
    plane(lambda device: send(gram_in.at[0], gram_all.at[tile], gram_batch, device))
    pltpu.make_async_copy(gram_in.at[0], gram_all.at[tile], recv_sem.at[gram_batch]).start()

    arrived(right_in.at[pl.ds(1, 2 * depth - 1)], RIGHT)
    right_all[strip] = right[strip] + jnp.sum(right_in[1:], axis=0)
    for k in far_row:
        send(right_all.at[strip], right_all.at[strip], RIGHT_ALL, (col, row_peer(k)))

    def fill(low, size):
        work[pl.ds(low, size), :LANES] = gram_all[pl.ds(low, size)]
        work[pl.ds(low, size), LANES:] = gram_all[pl.ds(RANK + low, size)]

    def fill_rest():
        arrived(gram_all.at[pl.ds(0, 2 * (RANK - panel_rows))], GRAM_REST)
        fill(panel_rows, RANK - panel_rows)

    arrived(gram_all.at[pl.ds(0, 2 * panel_rows)], GRAM_FIRST)
    fill(0, panel_rows)
    inverse_factor(work, panel_rows, 16, fill_rest)
    inverse = work[...]

    arrived(right_all.at[pl.ds(0, RANK - strip_rows)], RIGHT_ALL)
    raw = dot(right_all[...], inverse, 1, 1)
    sums = jnp.sum(raw * raw, axis=0, keepdims=True)
    squares[0:1] = sums[:, :LANES]
    squares[1:2] = sums[:, LANES:]
    squares_in[col] = squares[...]
    plane(lambda device: send(squares, squares_in.at[col], SQUARES, device))

    right_raw[...] = raw
    left_factor[...] = dot(left_raw, inverse, 1, 1)
    new_momentum[...] = combined[...] - 0.05 * dot(left_factor[...], raw, 1, 1)
    loads[3].wait()

    sent(scatter_in.at[0, pl.ds(1, side - 1), pl.ds(0, half)], FAR_X)
    sent(scatter_in.at[0, pl.ds(1, side - 1), pl.ds(0, half)], NEAR_X)
    sent(scatter_in.at[1, pl.ds(1, side - 1), pl.ds(0, half)], FAR_Z)
    sent(scatter_in.at[1, pl.ds(1, side - 1), pl.ds(0, half)], NEAR_Z)
    sent(middle_in.at[0, pl.ds(1, side - 1)], IN_Z)
    sent(middle_in.at[1, pl.ds(1, side - 1)], IN_X)
    for g in range(len(groups)):
        if count(g):
            sent(middle_in.at[0, pl.ds(0, count(g))], BACK_Z + g)
            sent(middle_in.at[1, pl.ds(0, count(g))], BACK_X + g)
    sent(gathered.at[0, pl.ds(1, side - 1)], ALL_X)
    sent(gathered.at[1, pl.ds(1, side - 1)], ALL_Z)
    sent(gram_in.at[pl.ds(0, 2 * depth - 1)], GRAM)
    sent(gram_all.at[pl.ds(0, 2 * RANK - tile_rows)], gram_batch)
    sent(right_in.at[pl.ds(1, 2 * depth - 1)], RIGHT)
    sent(right_all.at[pl.ds(0, RANK - strip_rows)], RIGHT_ALL)

    arrived(squares_in.at[pl.ds(0, side * side - 1)], SQUARES)
    total[...] = jnp.sum(squares_in[...], axis=0)
    sent(squares_in.at[pl.ds(0, side * side - 1)], SQUARES)


def finish(
    weight, momentum_now, left_factor, right_raw, total, new_weight_hbm, new_momentum_hbm, new_factor_hbm,
    new_weight, new_factor, store_sem,
):
    store_momentum = pltpu.make_async_copy(momentum_now, new_momentum_hbm, store_sem.at[0])
    store_momentum.start()
    sums = jnp.concatenate([total[0:1], total[1:2]], axis=1)
    new_factor[...] = right_raw[...] / jnp.sqrt(sums / D_IN + 1e-06)
    store_factor = pltpu.make_async_copy(new_factor, new_factor_hbm, store_sem.at[1])
    store_factor.start()
    parts = 2
    size = weight.shape[0] // parts
    stores = []
    for part in range(parts):
        block = pl.ds(part * size, size)
        new_weight[block] = weight[block] - 0.5 * dot(left_factor[block], new_factor[...], 1, 1)
        stores.append(
            pltpu.make_async_copy(new_weight.at[block], new_weight_hbm.at[block], store_sem.at[2 + part])
        )
        stores[-1].start()
    store_momentum.wait()
    store_factor.wait()
    for store in stores:
        store.wait()


def on_device(side, depth, weight, momentum, gradient, right_factor):
    rows, columns = weight.shape
    small = rows // side // side
    tile_rows = 2 * RANK // (side * side)
    vmem = pltpu.VMEM
    tiles = (side, side, small, LANES)
    big = jax.ShapeDtypeStruct((rows, columns), F32)
    tall = jax.ShapeDtypeStruct((rows, RANK), F32)
    square = jax.ShapeDtypeStruct((columns, RANK), F32)
    scratch = [
        vmem((rows, columns), F32),
        vmem((rows, columns), gradient.dtype),
        vmem((columns, RANK), F32),
        vmem((rows, columns), F32),
        vmem((2, *tiles), F32),
        vmem((2, *tiles), F32),
        vmem((2, *tiles), F32),
        vmem((2, side, small, LANES), F32),
        vmem((2, side, small, LANES), F32),
        vmem((2, *tiles), F32),
        vmem((2, *tiles), F32),
        vmem((LANES, LANES), F32),
        vmem((2 * depth, tile_rows, LANES), F32),
        vmem((2 * RANK, LANES), F32),
        vmem((RANK, RANK), F32),
        vmem((columns, RANK), F32),
        vmem((2 * depth, columns // (2 * depth), RANK), F32),
        vmem((columns, RANK), F32),
        vmem((2, LANES), F32),
        vmem((side * side, 2, LANES), F32),
        pltpu.SemaphoreType.DMA((4,)),
        pltpu.SemaphoreType.DMA((BATCHES,)),
        pltpu.SemaphoreType.DMA((BATCHES,)),
    ]
    arguments = [pltpu.with_memory_space_constraint(a, pltpu.HBM) for a in (weight, momentum, gradient, right_factor)]
    middle = pl.pallas_call(
        functools.partial(kernel, side, depth),
        out_shape=(big, big, tall, square, jax.ShapeDtypeStruct((2, LANES), F32)),
        in_specs=[pl.BlockSpec(memory_space=pl.ANY)] * 4,
        out_specs=(pl.BlockSpec(memory_space=vmem),) * 5,
        scratch_shapes=scratch,
        compiler_params=pltpu.CompilerParams(
            collective_id=0, has_side_effects=True, vmem_limit_bytes=24 * 1024 * 1024
        ),
        name="dion_step",
    )(*arguments)
    return pl.pallas_call(
        finish,
        out_shape=(big, big, square),
        in_specs=[pl.BlockSpec(memory_space=vmem)] * 5,
        out_specs=(pl.BlockSpec(memory_space=pl.ANY),) * 3,
        scratch_shapes=[vmem((rows, columns), F32), vmem((columns, RANK), F32), pltpu.SemaphoreType.DMA((4,))],
        compiler_params=pltpu.CompilerParams(vmem_limit_bytes=24 * 1024 * 1024),
        name="dion_finish",
    )(*middle)


def solution(mesh):
    side = math.isqrt(mesh.shape["col"])
    depth = mesh.shape["row"] // 2
    in_specs = (P("row", "col"), P("row", "col"), P("row", "col"), P("col", None))
    out_specs = (P("row", "col"), P("row", "col"), P("col", None))
    return jax.shard_map(
        functools.partial(on_device, side, depth), mesh=mesh, in_specs=in_specs, out_specs=out_specs, check_vma=False
    )
```

```python
import functools
import math

import jax
import jax.numpy as jnp
from jax import lax
from jax.experimental import pallas as pl
from jax.experimental.pallas import tpu as pltpu
from jax.sharding import PartitionSpec as P

D_IN = 16384
RANK = 256
LANES = 128
MESH = pl.DeviceIdType.MESH
F32 = jnp.float32

OUT_X, OUT_Z, BACK_X, BACK_Z = 0, 4, 8, 12
IN_X, IN_Z, ALL_X, ALL_Z, GRAM, GRAM_FIRST, GRAM_REST, PAIR, RIGHT, RIGHT_ALL, SQUARES, BATCHES = range(16, 28)


def dot(first, second, first_dim, second_dim):
    return lax.dot_general(
        first,
        second,
        (((first_dim,), (second_dim,)), ((), ())),
        precision=lax.Precision.HIGHEST,
        preferred_element_type=F32,
    )


def iota(shape, dim):
    return lax.broadcasted_iota(jnp.int32, shape, dim)


def eliminate(panel, first, inner):
    block, n = panel.shape
    copies = n // LANES

    def spread(column, r):
        return jnp.broadcast_to(column[r // 8, r % 8 : r % 8 + 1, :], (8, LANES))

    done = []
    for start in range(0, block, inner):
        rows = panel.shape[0]
        low = first + start
        columns = [
            jnp.broadcast_to(panel[:, low + j : low + j + 1], (rows, LANES)).reshape(rows // 8, 8, LANES)
            for j in range(inner)
        ]
        lane, sub = iota((rows, n), 1), iota((rows, n), 0)
        identity = jnp.where(lane - low == sub, 1.0, 0.0)
        panel = jnp.where((lane >= low) & (lane < low + inner), identity, panel)
        pivot = spread(columns[0], 0)
        scales, dropped = [], 0
        for j in range(inner):
            r = j - dropped
            scale = lax.rsqrt(pivot)
            scales.append(scale[:1])
            if j + 1 < inner:
                side = spread(columns[j], r + 1) * scale
                pivot = spread(columns[j + 1], r + 1) - side * side
            scaled = columns[j] * scale[None]
            for later in range(j + 1, inner):
                columns[later] = columns[later] - scaled * (spread(columns[later], r) * scale)[None]
            live = panel.shape[0]
            factor = (scaled * scale[None]).reshape(live, LANES)
            factor = jnp.where(iota((live, LANES), 0) > r, factor, 0.0)
            factor = jnp.concatenate([factor] * copies, axis=1)
            panel = panel - factor * jnp.broadcast_to(panel[r : r + 1, :], (live, n))
            if r == 7:
                all_scales = jnp.concatenate(scales, axis=0)
                done.append(panel[:8] * jnp.concatenate([all_scales] * copies, axis=1))
                panel = panel[8:]
                columns = [c[1:] if i > j else c for i, c in enumerate(columns)]
                scales, dropped = [], dropped + 8
    return jnp.concatenate(done, axis=0)


def inverse_factor(work, fill_rest):
    n = work.shape[0]
    half, block = n // 2, n // 4

    def swapped(value):
        return jnp.concatenate([value[:, half:], value[:, :half]], axis=1)

    def step(index, carry):
        lane, sub = iota((block, n), 1), iota((block, n), 0)
        upper = eliminate(work[0:block, :], 0, 16)
        pl.when(index == 0)(fill_rest)
        own_part = jnp.where((lane < block) & (lane > sub), 0.0, upper)
        lower = jnp.where(lane < block, 0.0, work[block:half, :]) - dot(upper[:, block:half], own_part, 0, 0)
        lower = eliminate(lower, block, 16)
        both = jnp.concatenate([upper, lower], axis=0)
        lane, sub = iota((half, n), 1), iota((half, n), 0)
        ready = swapped(jnp.where((lane > sub) & (lane < n - half * index), 0.0, both))

        @pl.when(index == 0)
        def _():
            own_part = jnp.where((lane < half) & (lane > sub), 0.0, both)
            rest = jnp.where(lane < half, 0.0, work[half:, :]) - dot(both[:, half:], own_part, 0, 0)
            work[0:half, :] = swapped(rest)

        @pl.when(index == 1)
        def _():
            work[0:half, :] = swapped(work[half:, :])

        work[half:, :] = ready
        return carry

    lax.fori_loop(0, 2, step, 0)


def kernel(
    side, depth, weight_hbm, momentum_hbm, gradient_hbm, factor_hbm,
    weight, new_momentum, left_factor, right_raw, total,
    momentum, gradient, factor, combined, product, partial, scatter_in, middle, middle_in, gathered, left, gram, gram_in,
    gram_all, work, right, pair_in, right_in, right_all, squares, squares_in, load_sem, send_sem, recv_sem,
):
    col, row = lax.axis_index("col"), lax.axis_index("row")
    z, x = lax.div(col, side), lax.rem(col, side)
    here, half = (x, z), side // 2
    offsets = sorted(range(side), key=lambda k: min(k, side - k))
    groups = [
        [slot for slot, k in enumerate(offsets) if min(k, side - k, 3) == distance] for distance in range(4)
    ]
    groups = [(slots[0], len(slots)) for slots in groups if slots]
    far = sorted(range(1, side), key=lambda k: -min(k, side - k))
    far_row = sorted(range(1, 2 * depth), key=lambda k: -min(k // 2, depth - k // 2))

    def x_peer(k):
        return at(z, lax.rem(x + k, side))

    def z_peer(k):
        return at(lax.rem(z + k, side), x)

    def at(z_of, x_of):
        return (z_of * side + x_of, row)

    def row_peer(k):
        return lax.rem(row + k, 2 * depth)

    def send(source, target, batch, device):
        pltpu.make_async_remote_copy(
            src_ref=source,
            dst_ref=target,
            send_sem=send_sem.at[batch],
            recv_sem=recv_sem.at[batch],
            device_id=device,
            device_id_type=MESH,
        ).start()

    def arrived(target, batch):
        pltpu.make_async_copy(target, target, recv_sem.at[batch]).wait()

    def sent(source, batch):
        pltpu.make_async_copy(source, source, send_sem.at[batch]).wait()

    barrier = pltpu.get_barrier_semaphore()
    for k in far:
        pl.semaphore_signal(barrier, inc=1, device_id=x_peer(k), device_id_type=MESH)
        pl.semaphore_signal(barrier, inc=1, device_id=z_peer(k), device_id_type=MESH)
    for k in far_row:
        pl.semaphore_signal(barrier, inc=1, device_id=(col, row_peer(k)), device_id_type=MESH)

    loads = [
        pltpu.make_async_copy(source, target, load_sem.at[i])
        for i, (source, target) in enumerate(
            ((momentum_hbm, momentum), (gradient_hbm, gradient), (factor_hbm, factor), (weight_hbm, weight))
        )
    ]
    for load in loads:
        load.start()
    for load in loads[:3]:
        load.wait()
    combined[...] = momentum[...] + gradient[...].astype(F32)
    whole = dot(combined[...], factor[...], 1, 0)
    tiles = product.shape[1:]
    product[0] = whole[:, :LANES].reshape(tiles)
    product[1] = whole[:, LANES:].reshape(tiles)

    def place(part, slot):
        return lax.rem(here[1 - part] + offsets[slot], side)

    for slot in range(side):
        partial[0, :, slot] = product[0, :, place(0, slot)]
        partial[1, slot] = product[1, place(1, slot)]

    pl.semaphore_wait(barrier, 2 * len(far) + len(far_row))

    for g, (low, size) in reversed(list(enumerate(groups))):
        tiles = pl.ds(low, size)
        for k in far:
            send(partial.at[0, lax.rem(x + k, side), tiles], scatter_in.at[0, k, tiles], OUT_X + g, x_peer(k))
            send(partial.at[1, tiles, lax.rem(z + k, side)], scatter_in.at[1, k, tiles], OUT_Z + g, z_peer(k))
    for g, (low, size) in reversed(list(enumerate(groups))):
        tiles = pl.ds(low, size)
        for part, batch, onward, peer in ((0, OUT_X, IN_Z, z_peer), (1, OUT_Z, IN_X, x_peer)):
            arrived(scatter_in.at[part, pl.ds(1, side - 1), tiles], batch + g)
            own = partial[0, x, tiles] if part == 0 else partial[1, tiles, z]
            middle[part, tiles] = own + jnp.sum(scatter_in[part, 1:, tiles], axis=0)
            for slot in reversed(range(low, low + size)):
                k = offsets[slot]
                if k:
                    send(middle.at[part, slot], middle_in.at[part, k], onward, peer(k))

    def forward(g, part):
        batch, peer = ((ALL_X, x_peer), (ALL_Z, z_peer))[part]
        block = gathered.at[part, here[part], pl.ds(*groups[g])]
        for k in far:
            send(block, block, batch, peer(k))

    group_of = [g for g, (low, size) in enumerate(groups) for _ in range(size)]
    for part, batch, back, peer in ((0, IN_Z, BACK_Z, z_peer), (1, IN_X, BACK_X, x_peer)):
        arrived(middle_in.at[part, pl.ds(1, side - 1)], batch)
        own = gathered.at[part, here[part], 0]
        own[...] = middle[part, 0] + jnp.sum(middle_in[part, 1:], axis=0)
        for k in far:
            slot = offsets.index(side - k)
            send(own, gathered.at[part, here[part], slot], back + group_of[slot], peer(k))
        forward(0, part)
    for g in range(1, len(groups)):
        for part, back in ((0, BACK_Z), (1, BACK_X)):
            arrived(middle_in.at[part, pl.ds(0, groups[g][1])], back + g)
            forward(g, part)
    arrived(gathered.at[0, pl.ds(1, side - 1)], ALL_X)
    arrived(gathered.at[1, pl.ds(1, side - 1)], ALL_Z)
    for slot in range(side):
        left[0, :, place(0, slot)] = gathered[0, :, slot]
        left[1, place(1, slot)] = gathered[1, :, slot]

    rows = combined.shape[0]
    halves = [left[part].reshape(rows, LANES) for part in range(2)]
    left_raw = jnp.concatenate(halves, axis=1)
    tile_rows = 2 * RANK // (side * side)
    tile = pl.ds(col * tile_rows, tile_rows)
    start = col * tile_rows
    block_row = lax.rem(lax.div(start, LANES), 2)
    block_col = lax.div(start, RANK)
    gram[...] = dot(left[block_row].reshape(rows, LANES), left[block_col].reshape(rows, LANES), 0, 0)
    own_tile = pl.ds(lax.rem(start, LANES), tile_rows)
    gram_in[row] = gram[own_tile]
    used = (block_row == 0) | (block_col == 1)

    @pl.when(used)
    def _():
        for k in far_row:
            send(gram.at[own_tile], gram_in.at[row], GRAM, (col, row_peer(k)))

    core, y = lax.rem(row, 2), lax.div(row, 2)
    pair_rows = RANK // 2
    right[...] = dot(combined[...], left_raw, 0, 0)
    send(right.at[pl.ds((1 - core) * pair_rows, pair_rows)], pair_in, PAIR, (col, row + 1 - 2 * core))
    arrived(pair_in, PAIR)
    mine = pl.ds(core * pair_rows, pair_rows)
    right[mine] = right[mine] + pair_in[...]

    strip_rows = pair_rows // depth

    def strip_of(y_of):
        return pl.ds(core * pair_rows + y_of * strip_rows, strip_rows)

    for k in sorted(range(1, depth), key=lambda k: -min(k, depth - k)):
        y_peer = lax.rem(y + k, depth)
        send(right.at[strip_of(y_peer)], right_in.at[k], RIGHT, (col, 2 * y_peer + core))

    def plane(start):
        def one(j, carry):
            dz, dx = far_of(lax.div(j, side)), far_of(lax.rem(j, side))
            start(at(lax.rem(z + dz, side), lax.rem(x + dx, side)))
            return carry

        lax.fori_loop(0, side * side - 1, one, 0)

    def far_of(j):
        step = lax.div(j + 1, 2)
        return half + jnp.where(lax.rem(j, 2) == 1, -step, step)

    panel_rows = RANK // 4
    first = lax.rem(start, RANK) < panel_rows
    gram_batch = jnp.where(first, GRAM_FIRST, GRAM_REST)

    @pl.when(used)
    def _():
        arrived(gram_in.at[pl.ds(0, 2 * depth - 1)], GRAM)
        gram_in[0] = jnp.sum(gram_in[...], axis=0)
        plane(lambda device: send(gram_in.at[0], gram_all.at[tile], gram_batch, device))
        pltpu.make_async_copy(gram_in.at[0], gram_all.at[tile], recv_sem.at[gram_batch]).start()

    strip = strip_of(y)
    if depth > 1:
        arrived(right_in.at[pl.ds(1, depth - 1)], RIGHT)
    right_all[strip] = right[strip] + jnp.sum(right_in[1:], axis=0)
    for k in far_row:
        send(right_all.at[strip], right_all.at[strip], RIGHT_ALL, (col, row_peer(k)))

    def fill_rest():
        arrived(gram_all.at[pl.ds(0, 2 * (RANK - panel_rows) - LANES)], GRAM_REST)
        work[panel_rows:LANES, :LANES] = gram_all[panel_rows:LANES]
        work[panel_rows:, LANES:] = gram_all[RANK + panel_rows :]

    arrived(gram_all.at[pl.ds(0, 2 * panel_rows)], GRAM_FIRST)
    work[0:panel_rows, :LANES] = gram_all[0:panel_rows]
    work[0:panel_rows, LANES:] = gram_all[RANK : RANK + panel_rows]
    work[LANES:, :LANES] = jnp.zeros((RANK - LANES, LANES), F32)
    inverse_factor(work, fill_rest)
    inverse = work[...]

    arrived(right_all.at[pl.ds(0, RANK - strip_rows)], RIGHT_ALL)
    raw = dot(right_all[...], inverse, 1, 1)
    sums = jnp.sum(raw * raw, axis=0, keepdims=True)
    squares[0:1] = sums[:, :LANES]
    squares[1:2] = sums[:, LANES:]
    squares_in[col] = squares[...]
    plane(lambda device: send(squares, squares_in.at[col], SQUARES, device))

    right_raw[...] = raw
    left_factor[...] = dot(left_raw, inverse, 1, 1)
    new_momentum[...] = combined[...] - 0.05 * dot(left_factor[...], raw, 1, 1)
    loads[3].wait()

    for g, (low, size) in enumerate(groups):
        for part, out, back in ((0, OUT_X, BACK_Z), (1, OUT_Z, BACK_X)):
            sent(scatter_in.at[part, pl.ds(1, side - 1), pl.ds(0, size)], out + g)
            if g:
                sent(middle_in.at[part, pl.ds(0, size)], back + g)
    sent(middle_in.at[0, pl.ds(1, side - 1)], IN_Z)
    sent(middle_in.at[1, pl.ds(1, side - 1)], IN_X)
    sent(gathered.at[0, pl.ds(1, side - 1)], ALL_X)
    sent(gathered.at[1, pl.ds(1, side - 1)], ALL_Z)

    @pl.when(used)
    def _():
        sent(gram_in.at[pl.ds(0, 2 * depth - 1)], GRAM)
        sent(gram_all.at[pl.ds(0, 2 * RANK - tile_rows)], gram_batch)

    sent(pair_in, PAIR)
    if depth > 1:
        sent(right_in.at[pl.ds(1, depth - 1)], RIGHT)
    sent(right_all.at[pl.ds(0, RANK - strip_rows)], RIGHT_ALL)

    arrived(squares_in.at[pl.ds(0, side * side - 1)], SQUARES)
    total[...] = jnp.sum(squares_in[...], axis=0)
    sent(squares_in.at[pl.ds(0, side * side - 1)], SQUARES)


def finish(
    weight, momentum_now, left_factor, right_raw, total, new_weight_hbm, new_momentum_hbm, new_factor_hbm,
    new_weight, new_factor, store_sem,
):
    store_momentum = pltpu.make_async_copy(momentum_now, new_momentum_hbm, store_sem.at[0])
    store_momentum.start()
    sums = jnp.concatenate([total[0:1], total[1:2]], axis=1)
    new_factor[...] = right_raw[...] / jnp.sqrt(sums / D_IN + 1e-06)
    store_factor = pltpu.make_async_copy(new_factor, new_factor_hbm, store_sem.at[1])
    store_factor.start()
    parts = 2
    size = weight.shape[0] // parts
    stores = []
    for part in range(parts):
        block = pl.ds(part * size, size)
        new_weight[block] = weight[block] - 0.5 * dot(left_factor[block], new_factor[...], 1, 1)
        stores.append(
            pltpu.make_async_copy(new_weight.at[block], new_weight_hbm.at[block], store_sem.at[2 + part])
        )
        stores[-1].start()
    store_momentum.wait()
    store_factor.wait()
    for store in stores:
        store.wait()


def on_device(side, depth, weight, momentum, gradient, right_factor):
    rows, columns = weight.shape
    small = rows // side // side
    tile_rows = 2 * RANK // (side * side)
    vmem = pltpu.VMEM
    tiles = (side, side, small, LANES)
    big = jax.ShapeDtypeStruct((rows, columns), F32)
    tall = jax.ShapeDtypeStruct((rows, RANK), F32)
    square = jax.ShapeDtypeStruct((columns, RANK), F32)
    scratch = [
        vmem((rows, columns), F32),
        vmem((rows, columns), gradient.dtype),
        vmem((columns, RANK), F32),
        vmem((rows, columns), F32),
        vmem((2, *tiles), F32),
        vmem((2, *tiles), F32),
        vmem((2, *tiles), F32),
        vmem((2, side, small, LANES), F32),
        vmem((2, side, small, LANES), F32),
        vmem((2, *tiles), F32),
        vmem((2, *tiles), F32),
        vmem((LANES, LANES), F32),
        vmem((2 * depth, tile_rows, LANES), F32),
        vmem((2 * RANK, LANES), F32),
        vmem((RANK, RANK), F32),
        vmem((columns, RANK), F32),
        vmem((columns // 2, RANK), F32),
        vmem((depth, columns // (2 * depth), RANK), F32),
        vmem((columns, RANK), F32),
        vmem((2, LANES), F32),
        vmem((side * side, 2, LANES), F32),
        pltpu.SemaphoreType.DMA((4,)),
        pltpu.SemaphoreType.DMA((BATCHES,)),
        pltpu.SemaphoreType.DMA((BATCHES,)),
    ]
    arguments = [pltpu.with_memory_space_constraint(a, pltpu.HBM) for a in (weight, momentum, gradient, right_factor)]
    middle = pl.pallas_call(
        functools.partial(kernel, side, depth),
        out_shape=(big, big, tall, square, jax.ShapeDtypeStruct((2, LANES), F32)),
        in_specs=[pl.BlockSpec(memory_space=pl.ANY)] * 4,
        out_specs=(pl.BlockSpec(memory_space=vmem),) * 5,
        scratch_shapes=scratch,
        compiler_params=pltpu.CompilerParams(
            collective_id=0, has_side_effects=True, vmem_limit_bytes=24 * 1024 * 1024
        ),
        name="dion_step",
    )(*arguments)
    return pl.pallas_call(
        finish,
        out_shape=(big, big, square),
        in_specs=[pl.BlockSpec(memory_space=vmem)] * 5,
        out_specs=(pl.BlockSpec(memory_space=pl.ANY),) * 3,
        scratch_shapes=[vmem((rows, columns), F32), vmem((columns, RANK), F32), pltpu.SemaphoreType.DMA((4,))],
        compiler_params=pltpu.CompilerParams(vmem_limit_bytes=24 * 1024 * 1024),
        name="dion_finish",
    )(*middle)


def solution(mesh):
    side = math.isqrt(mesh.shape["col"])
    depth = mesh.shape["row"] // 2
    in_specs = (P("row", "col"), P("row", "col"), P("row", "col"), P("col", None))
    out_specs = (P("row", "col"), P("row", "col"), P("col", None))
    return jax.shard_map(
        functools.partial(on_device, side, depth), mesh=mesh, in_specs=in_specs, out_specs=out_specs, check_vma=False
    )
```

```python
import functools
import math

import jax
import jax.numpy as jnp
from jax import lax
from jax.experimental import pallas as pl
from jax.experimental.pallas import tpu as pltpu
from jax.sharding import PartitionSpec as P

D_IN = 16384
RANK = 256
LANES = 128
MESH = pl.DeviceIdType.MESH
F32 = jnp.float32

OUT_X, OUT_Z, BACK_X, BACK_Z = 0, 4, 8, 12
IN_X, IN_Z, ALL_X, ALL_Z, GRAM, GRAM_FIRST, GRAM_REST, PAIR, RIGHT, RIGHT_ALL, SQUARES, BATCHES = range(16, 28)


def dot(first, second, first_dim, second_dim):
    return lax.dot_general(
        first,
        second,
        (((first_dim,), (second_dim,)), ((), ())),
        precision=lax.Precision.HIGHEST,
        preferred_element_type=F32,
    )


def iota(shape, dim):
    return lax.broadcasted_iota(jnp.int32, shape, dim)


def eliminate(panel, first, inner):
    block, n = panel.shape
    copies = n // LANES

    def spread(column, r):
        return jnp.broadcast_to(column[r // 8, r % 8 : r % 8 + 1, :], (8, LANES))

    done = []
    for start in range(0, block, inner):
        rows = panel.shape[0]
        low = first + start
        columns = [
            jnp.broadcast_to(panel[:, low + j : low + j + 1], (rows, LANES)).reshape(rows // 8, 8, LANES)
            for j in range(inner)
        ]
        lane, sub = iota((rows, n), 1), iota((rows, n), 0)
        identity = jnp.where(lane - low == sub, 1.0, 0.0)
        panel = jnp.where((lane >= low) & (lane < low + inner), identity, panel)
        pivot = spread(columns[0], 0)
        scales, dropped = [], 0
        for j in range(inner):
            r = j - dropped
            scale = lax.rsqrt(pivot)
            scales.append(scale[:1])
            if j + 1 < inner:
                side = spread(columns[j], r + 1) * scale
                pivot = spread(columns[j + 1], r + 1) - side * side
            scaled = columns[j] * scale[None]
            for later in range(j + 1, inner):
                columns[later] = columns[later] - scaled * (spread(columns[later], r) * scale)[None]
            live = panel.shape[0]
            factor = (scaled * scale[None]).reshape(live, LANES)
            factor = jnp.where(iota((live, LANES), 0) > r, factor, 0.0)
            factor = jnp.concatenate([factor] * copies, axis=1)
            panel = panel - factor * jnp.broadcast_to(panel[r : r + 1, :], (live, n))
            if r == 7:
                all_scales = jnp.concatenate(scales, axis=0)
                done.append(panel[:8] * jnp.concatenate([all_scales] * copies, axis=1))
                panel = panel[8:]
                columns = [c[1:] if i > j else c for i, c in enumerate(columns)]
                scales, dropped = [], dropped + 8
    return jnp.concatenate(done, axis=0)


def inverse_factor(work, fill_rest):
    n = work.shape[0]
    half, block = n // 2, n // 4

    def swapped(value):
        return jnp.concatenate([value[:, half:], value[:, :half]], axis=1)

    def step(index, carry):
        lane, sub = iota((block, n), 1), iota((block, n), 0)
        upper = eliminate(work[0:block, :], 0, 16)
        pl.when(index == 0)(fill_rest)
        own_part = jnp.where((lane < block) & (lane > sub), 0.0, upper)
        lower = jnp.where(lane < block, 0.0, work[block:half, :]) - dot(upper[:, block:half], own_part, 0, 0)
        lower = eliminate(lower, block, 16)
        both = jnp.concatenate([upper, lower], axis=0)
        lane, sub = iota((half, n), 1), iota((half, n), 0)
        ready = swapped(jnp.where((lane > sub) & (lane < n - half * index), 0.0, both))

        @pl.when(index == 0)
        def _():
            own_part = jnp.where((lane < half) & (lane > sub), 0.0, both)
            rest = jnp.where(lane < half, 0.0, work[half:, :]) - dot(both[:, half:], own_part, 0, 0)
            work[0:half, :] = swapped(rest)

        @pl.when(index == 1)
        def _():
            work[0:half, :] = swapped(work[half:, :])

        work[half:, :] = ready
        return carry

    lax.fori_loop(0, 2, step, 0)


def kernel(
    side, depth, weight_hbm, momentum_hbm, gradient_hbm, factor_hbm,
    weight, new_momentum, left_factor, right_raw, total,
    momentum, gradient, factor, combined, product, partial, scatter_in, middle, middle_in, gathered, left, gram, gram_in,
    gram_all, work, right, pair_in, right_in, right_all, squares, squares_in, load_sem, send_sem, recv_sem,
):
    col, row = lax.axis_index("col"), lax.axis_index("row")
    z, x = lax.div(col, side), lax.rem(col, side)
    here, half = (x, z), side // 2
    offsets = sorted(range(side), key=lambda k: min(k, side - k))
    groups = [
        [slot for slot, k in enumerate(offsets) if min(k, side - k, 3) == distance] for distance in range(4)
    ]
    groups = [(slots[0], len(slots)) for slots in groups if slots]
    far = sorted(range(1, side), key=lambda k: -min(k, side - k))
    far_row = sorted(range(1, 2 * depth), key=lambda k: -min(k // 2, depth - k // 2))

    def x_peer(k):
        return at(z, lax.rem(x + k, side))

    def z_peer(k):
        return at(lax.rem(z + k, side), x)

    def at(z_of, x_of):
        return (z_of * side + x_of, row)

    def row_peer(k):
        return lax.rem(row + k, 2 * depth)

    def send(source, target, batch, device):
        pltpu.make_async_remote_copy(
            src_ref=source,
            dst_ref=target,
            send_sem=send_sem.at[batch],
            recv_sem=recv_sem.at[batch],
            device_id=device,
            device_id_type=MESH,
        ).start()

    def arrived(target, batch):
        pltpu.make_async_copy(target, target, recv_sem.at[batch]).wait()

    def sent(source, batch):
        pltpu.make_async_copy(source, source, send_sem.at[batch]).wait()

    barrier = pltpu.get_barrier_semaphore()
    greeted = [(min(k, side - k), peer(k)) for k in far for peer in (x_peer, z_peer)]
    greeted += [(min(k // 2, depth - k // 2), (col, row_peer(k))) for k in far_row]
    for _, device in sorted(greeted, key=lambda entry: -entry[0]):
        pl.semaphore_signal(barrier, inc=1, device_id=device, device_id_type=MESH)

    loads = [
        pltpu.make_async_copy(source, target, load_sem.at[i])
        for i, (source, target) in enumerate(
            ((momentum_hbm, momentum), (gradient_hbm, gradient), (factor_hbm, factor), (weight_hbm, weight))
        )
    ]
    for load in loads:
        load.start()
    for load in loads[:3]:
        load.wait()
    combined[...] = momentum[...] + gradient[...].astype(F32)
    whole = dot(combined[...], factor[...], 1, 0)
    tiles = product.shape[1:]
    product[0] = whole[:, :LANES].reshape(tiles)
    product[1] = whole[:, LANES:].reshape(tiles)

    def place(part, slot):
        return lax.rem(here[1 - part] + offsets[slot], side)

    for slot in range(side):
        partial[0, :, slot] = product[0, :, place(0, slot)]
        partial[1, slot] = product[1, place(1, slot)]

    pl.semaphore_wait(barrier, 2 * len(far) + len(far_row))

    for g, (low, size) in reversed(list(enumerate(groups))):
        tiles = pl.ds(low, size)
        for k in far:
            send(partial.at[0, lax.rem(x + k, side), tiles], scatter_in.at[0, k, tiles], OUT_X + g, x_peer(k))
            send(partial.at[1, tiles, lax.rem(z + k, side)], scatter_in.at[1, k, tiles], OUT_Z + g, z_peer(k))
    for g, (low, size) in reversed(list(enumerate(groups))):
        tiles = pl.ds(low, size)
        for part, batch, onward, peer in ((0, OUT_X, IN_Z, z_peer), (1, OUT_Z, IN_X, x_peer)):
            arrived(scatter_in.at[part, pl.ds(1, side - 1), tiles], batch + g)
            own = partial[0, x, tiles] if part == 0 else partial[1, tiles, z]
            middle[part, tiles] = own + jnp.sum(scatter_in[part, 1:, tiles], axis=0)
            for slot in reversed(range(low, low + size)):
                k = offsets[slot]
                if k:
                    send(middle.at[part, slot], middle_in.at[part, k], onward, peer(k))

    def forward(g, part):
        batch, peer = ((ALL_X, x_peer), (ALL_Z, z_peer))[part]
        block = gathered.at[part, here[part], pl.ds(*groups[g])]
        for k in far:
            send(block, block, batch, peer(k))

    group_of = [g for g, (low, size) in enumerate(groups) for _ in range(size)]
    for part, batch, back, peer in ((0, IN_Z, BACK_Z, z_peer), (1, IN_X, BACK_X, x_peer)):
        arrived(middle_in.at[part, pl.ds(1, side - 1)], batch)
        own = gathered.at[part, here[part], 0]
        own[...] = middle[part, 0] + jnp.sum(middle_in[part, 1:], axis=0)
        for k in far:
            slot = offsets.index(side - k)
            send(own, gathered.at[part, here[part], slot], back + group_of[slot], peer(k))
        forward(0, part)
    for g in range(1, len(groups)):
        for part, back in ((0, BACK_Z), (1, BACK_X)):
            arrived(middle_in.at[part, pl.ds(0, groups[g][1])], back + g)
            forward(g, part)
    arrived(gathered.at[0, pl.ds(1, side - 1)], ALL_X)
    arrived(gathered.at[1, pl.ds(1, side - 1)], ALL_Z)
    for slot in range(side):
        left[0, :, place(0, slot)] = gathered[0, :, slot]
        left[1, place(1, slot)] = gathered[1, :, slot]

    rows = combined.shape[0]
    halves = [left[part].reshape(rows, LANES) for part in range(2)]
    left_raw = jnp.concatenate(halves, axis=1)
    tile_rows = 2 * RANK // (side * side)
    tile = pl.ds(col * tile_rows, tile_rows)
    start = col * tile_rows
    block_row = lax.rem(lax.div(start, LANES), 2)
    block_col = lax.div(start, RANK)
    gram[...] = dot(left[block_row].reshape(rows, LANES), left[block_col].reshape(rows, LANES), 0, 0)
    own_tile = pl.ds(lax.rem(start, LANES), tile_rows)
    gram_in[row] = gram[own_tile]
    used = (block_row == 0) | (block_col == 1)

    @pl.when(used)
    def _():
        for k in far_row:
            send(gram.at[own_tile], gram_in.at[row], GRAM, (col, row_peer(k)))

    core, y = lax.rem(row, 2), lax.div(row, 2)
    pair_rows = RANK // 2
    right[...] = dot(combined[...], left_raw, 0, 0)
    send(right.at[pl.ds((1 - core) * pair_rows, pair_rows)], pair_in, PAIR, (col, row + 1 - 2 * core))
    arrived(pair_in, PAIR)
    mine = pl.ds(core * pair_rows, pair_rows)
    right[mine] = right[mine] + pair_in[...]

    strip_rows = pair_rows // depth

    def strip_of(y_of):
        return pl.ds(core * pair_rows + y_of * strip_rows, strip_rows)

    for k in sorted(range(1, depth), key=lambda k: -min(k, depth - k)):
        y_peer = lax.rem(y + k, depth)
        send(right.at[strip_of(y_peer)], right_in.at[k], RIGHT, (col, 2 * y_peer + core))

    def plane(start):
        def one(j, carry):
            dz, dx = far_of(lax.div(j, side)), far_of(lax.rem(j, side))
            start(at(lax.rem(z + dz, side), lax.rem(x + dx, side)))
            return carry

        lax.fori_loop(0, side * side - 1, one, 0)

    def far_of(j):
        step = lax.div(j + 1, 2)
        return half + jnp.where(lax.rem(j, 2) == 1, -step, step)

    panel_rows = RANK // 4
    first = lax.rem(start, RANK) < panel_rows
    gram_batch = jnp.where(first, GRAM_FIRST, GRAM_REST)

    @pl.when(used)
    def _():
        arrived(gram_in.at[pl.ds(0, 2 * depth - 1)], GRAM)
        gram_in[0] = jnp.sum(gram_in[...], axis=0)
        plane(lambda device: send(gram_in.at[0], gram_all.at[tile], gram_batch, device))
        pltpu.make_async_copy(gram_in.at[0], gram_all.at[tile], recv_sem.at[gram_batch]).start()

    strip = strip_of(y)
    if depth > 1:
        arrived(right_in.at[pl.ds(1, depth - 1)], RIGHT)
    right_all[strip] = right[strip] + jnp.sum(right_in[1:], axis=0)
    for k in far_row:
        send(right_all.at[strip], right_all.at[strip], RIGHT_ALL, (col, row_peer(k)))

    def fill_rest():
        arrived(gram_all.at[pl.ds(0, 2 * (RANK - panel_rows) - LANES)], GRAM_REST)
        work[panel_rows:LANES, :LANES] = gram_all[panel_rows:LANES]
        work[panel_rows:, LANES:] = gram_all[RANK + panel_rows :]

    arrived(gram_all.at[pl.ds(0, 2 * panel_rows)], GRAM_FIRST)
    work[0:panel_rows, :LANES] = gram_all[0:panel_rows]
    work[0:panel_rows, LANES:] = gram_all[RANK : RANK + panel_rows]
    work[LANES:, :LANES] = jnp.zeros((RANK - LANES, LANES), F32)
    inverse_factor(work, fill_rest)
    inverse = work[...]

    arrived(right_all.at[pl.ds(0, RANK - strip_rows)], RIGHT_ALL)
    raw = dot(right_all[...], inverse, 1, 1)
    sums = jnp.sum(raw * raw, axis=0, keepdims=True)
    squares[0:1] = sums[:, :LANES]
    squares[1:2] = sums[:, LANES:]
    squares_in[col] = squares[...]
    plane(lambda device: send(squares, squares_in.at[col], SQUARES, device))

    right_raw[...] = raw
    left_factor[...] = dot(left_raw, inverse, 1, 1)
    new_momentum[...] = combined[...] - 0.05 * dot(left_factor[...], raw, 1, 1)
    loads[3].wait()

    for g, (low, size) in enumerate(groups):
        for part, out, back in ((0, OUT_X, BACK_Z), (1, OUT_Z, BACK_X)):
            sent(scatter_in.at[part, pl.ds(1, side - 1), pl.ds(0, size)], out + g)
            if g:
                sent(middle_in.at[part, pl.ds(0, size)], back + g)
    sent(middle_in.at[0, pl.ds(1, side - 1)], IN_Z)
    sent(middle_in.at[1, pl.ds(1, side - 1)], IN_X)
    sent(gathered.at[0, pl.ds(1, side - 1)], ALL_X)
    sent(gathered.at[1, pl.ds(1, side - 1)], ALL_Z)

    @pl.when(used)
    def _():
        sent(gram_in.at[pl.ds(0, 2 * depth - 1)], GRAM)
        sent(gram_all.at[pl.ds(0, 2 * RANK - tile_rows)], gram_batch)

    sent(pair_in, PAIR)
    if depth > 1:
        sent(right_in.at[pl.ds(1, depth - 1)], RIGHT)
    sent(right_all.at[pl.ds(0, RANK - strip_rows)], RIGHT_ALL)

    arrived(squares_in.at[pl.ds(0, side * side - 1)], SQUARES)
    total[...] = jnp.sum(squares_in[...], axis=0)
    sent(squares_in.at[pl.ds(0, side * side - 1)], SQUARES)


def finish(
    weight, momentum_now, left_factor, right_raw, total, new_weight_hbm, new_momentum_hbm, new_factor_hbm,
    new_weight, new_factor, store_sem,
):
    store_momentum = pltpu.make_async_copy(momentum_now, new_momentum_hbm, store_sem.at[0])
    store_momentum.start()
    sums = jnp.concatenate([total[0:1], total[1:2]], axis=1)
    new_factor[...] = right_raw[...] / jnp.sqrt(sums / D_IN + 1e-06)
    store_factor = pltpu.make_async_copy(new_factor, new_factor_hbm, store_sem.at[1])
    store_factor.start()
    parts = 2
    size = weight.shape[0] // parts
    stores = []
    for part in range(parts):
        block = pl.ds(part * size, size)
        new_weight[block] = weight[block] - 0.5 * dot(left_factor[block], new_factor[...], 1, 1)
        stores.append(
            pltpu.make_async_copy(new_weight.at[block], new_weight_hbm.at[block], store_sem.at[2 + part])
        )
        stores[-1].start()
    store_momentum.wait()
    store_factor.wait()
    for store in stores:
        store.wait()


def on_device(side, depth, weight, momentum, gradient, right_factor):
    rows, columns = weight.shape
    small = rows // side // side
    tile_rows = 2 * RANK // (side * side)
    vmem = pltpu.VMEM
    tiles = (side, side, small, LANES)
    big = jax.ShapeDtypeStruct((rows, columns), F32)
    tall = jax.ShapeDtypeStruct((rows, RANK), F32)
    square = jax.ShapeDtypeStruct((columns, RANK), F32)
    scratch = [
        vmem((rows, columns), F32),
        vmem((rows, columns), gradient.dtype),
        vmem((columns, RANK), F32),
        vmem((rows, columns), F32),
        vmem((2, *tiles), F32),
        vmem((2, *tiles), F32),
        vmem((2, *tiles), F32),
        vmem((2, side, small, LANES), F32),
        vmem((2, side, small, LANES), F32),
        vmem((2, *tiles), F32),
        vmem((2, *tiles), F32),
        vmem((LANES, LANES), F32),
        vmem((2 * depth, tile_rows, LANES), F32),
        vmem((2 * RANK, LANES), F32),
        vmem((RANK, RANK), F32),
        vmem((columns, RANK), F32),
        vmem((columns // 2, RANK), F32),
        vmem((depth, columns // (2 * depth), RANK), F32),
        vmem((columns, RANK), F32),
        vmem((2, LANES), F32),
        vmem((side * side, 2, LANES), F32),
        pltpu.SemaphoreType.DMA((4,)),
        pltpu.SemaphoreType.DMA((BATCHES,)),
        pltpu.SemaphoreType.DMA((BATCHES,)),
    ]
    arguments = [pltpu.with_memory_space_constraint(a, pltpu.HBM) for a in (weight, momentum, gradient, right_factor)]
    middle = pl.pallas_call(
        functools.partial(kernel, side, depth),
        out_shape=(big, big, tall, square, jax.ShapeDtypeStruct((2, LANES), F32)),
        in_specs=[pl.BlockSpec(memory_space=pl.ANY)] * 4,
        out_specs=(pl.BlockSpec(memory_space=vmem),) * 5,
        scratch_shapes=scratch,
        compiler_params=pltpu.CompilerParams(
            collective_id=0, has_side_effects=True, vmem_limit_bytes=24 * 1024 * 1024
        ),
        name="dion_step",
    )(*arguments)
    return pl.pallas_call(
        finish,
        out_shape=(big, big, square),
        in_specs=[pl.BlockSpec(memory_space=vmem)] * 5,
        out_specs=(pl.BlockSpec(memory_space=pl.ANY),) * 3,
        scratch_shapes=[vmem((rows, columns), F32), vmem((columns, RANK), F32), pltpu.SemaphoreType.DMA((4,))],
        compiler_params=pltpu.CompilerParams(vmem_limit_bytes=24 * 1024 * 1024),
        name="dion_finish",
    )(*middle)


def solution(mesh):
    side = math.isqrt(mesh.shape["col"])
    depth = mesh.shape["row"] // 2
    in_specs = (P("row", "col"), P("row", "col"), P("row", "col"), P("col", None))
    out_specs = (P("row", "col"), P("row", "col"), P("col", None))
    return jax.shard_map(
        functools.partial(on_device, side, depth), mesh=mesh, in_specs=in_specs, out_specs=out_specs, check_vma=False
    )
```
